32 devices in a mesh: groups: 2 (over x), member: 8 (over z, y), replica: 2 (over core).
Axes of the slice: x: 2, y: 2, z: 4, core: 2. Of those that a mesh axis runs over, the one named last changes fastest.
Arguments:
- states: bfloat16 [32768, 1536], P(('groups', 'member', 'replica')), parts along dimension 0, may hold values from -6 to 6
- rewards: float32 [32768], P(('groups', 'member', 'replica')), parts along dimension 0, may hold values from -6 to 6
- offsets: int32 [32768], P(('groups', 'member', 'replica')), parts along dimension 0, may hold values from 1 to 4
- blocks: int32 [32, 8], P(('groups', 'member', 'replica')), parts along dimension 0, may hold values from 0 to 15
- counts: int32 [16], P(('groups', 'member')), parts along dimension 0, may hold values from 64 to 1024, as said below
- w_first: bfloat16 [16, 1536, 1024], P(('groups', 'member')), parts along dimension 0, may hold values from -0.15625 to 0.15625
- b_first: bfloat16 [16, 1024], P(('groups', 'member')), parts along dimension 0, may hold values from -3 to 3
- w_value: bfloat16 [16, 1024], P(('groups', 'member')), parts along dimension 0, may hold values from -0.1875 to 0.1875
Outputs:
- grad_w1: bfloat16 [16, 1536, 1024], P(('groups', 'member')), parts along dimension 0
- grad_b1: float32 [16, 1024], P(('groups', 'member')), parts along dimension 0
- grad_w2: float32 [16, 1024], P(('groups', 'member')), parts along dimension 0
- td_error: float32 [32, 8, 64], P(('groups', 'member', 'replica')), parts along dimension 0
The draws below stay inside these ranges and needn't reach their ends.
There are 2 independent parts, one for each index of `groups`. The reference program is written for one: setup_inputs(seed, part) draws one part's arguments, and reference() takes and returns one part's arrays. A program takes and returns all parts, laid end to end along the dimension named above; each array names one. Nothing has to cross between parts.
Inputs may be any that keep to these rules, and one draw needn't show every extreme that they name: `counts`: some member uses all 1024 rows.
All inputs are finite; a program needn't handle non-finite values.
Results may differ from the reference program's by a relative error of at most 0.012.
Values may be sent and summed in bfloat16 or wider, within the bound.
A program may use at most 64 MiB of HBM per device.

```python
import jax
import jax.numpy as jnp
from jax import lax

D = 1536
H = 1024
PEER_ROWS = 64
ROLL_DEV = 1024
MEMBERS = 8
SHARDS = 16
BATCH = 1024
N_REPLICA = 2


def draw_counts(key, part):
    key = jax.random.fold_in(key, 7)
    first_key, second_key = jax.random.split(key)
    values = jax.random.randint(first_key, (MEMBERS,), PEER_ROWS, BATCH + 1)
    which = jax.random.randint(second_key, (), 0, MEMBERS)
    values = jnp.where(jnp.arange(MEMBERS) == which, BATCH, values)
    return values.astype(jnp.int32)


def place_ends(entries, own_key, smallest, high):
    spot = [jax.random.randint(jax.random.fold_in(own_key, axis), (), 0, length) for axis, length in enumerate(entries.shape)]
    main_axis = entries.shape.index(max(entries.shape))
    next_to = spot[:main_axis] + [(spot[main_axis] + 1) % entries.shape[main_axis]] + spot[main_axis + 1:]
    return entries.at[tuple(spot)].set(smallest).at[tuple(next_to)].set(high)


def steps_of(key, dims, pieces, low, largest):
    factor_of = 1.0
    for axis_at, shards_of in pieces:
        draws = jax.random.uniform(jax.random.fold_in(jax.random.fold_in(key, 6), axis_at), (shards_of,), jnp.float32, low / len(pieces), largest / len(pieces))
        factor_of = factor_of * jnp.repeat(jnp.exp(draws), dims[axis_at] // shards_of).reshape((-1,) + (1,) * (len(dims) - 1 - axis_at))
    return factor_of


def noise(stream_key, shape, deviation, most, pieces=(), kind=jnp.bfloat16):
    entries = jax.random.normal(stream_key, shape, jnp.float32) * deviation
    if len(pieces) > 0:
        entries = steps_of(stream_key, shape, pieces, -0.22, 0.18) * entries
    return jnp.clip(entries, min=-most, max=most).astype(kind)


def setup_inputs(seed: int = 0, part: int = 0) -> dict:
    key_of = jax.random.split(jax.random.key(seed), 9)
    part_keys = jax.random.split(jax.random.fold_in(key_of[8], part), 9)
    states = noise(part_keys[0], (SHARDS * ROLL_DEV, D), 1.0, 6.0, ((0, 16),))
    rewards = noise(part_keys[1], (SHARDS * ROLL_DEV,), 1.0, 6.0, ((0, 16),), jnp.float32)
    offsets = place_ends(jax.random.randint(part_keys[2], (SHARDS * ROLL_DEV,), 1, 5), jax.random.fold_in(part_keys[2], 1), 1, 4).astype(jnp.int32)
    blocks = place_ends(jax.random.randint(part_keys[3], (SHARDS, MEMBERS), 0, ROLL_DEV // PEER_ROWS), jax.random.fold_in(part_keys[3], 1), 0, (ROLL_DEV // PEER_ROWS) - 1).astype(jnp.int32)
    counts = draw_counts(jax.random.fold_in(jax.random.fold_in(key_of[8], part), 71), part)
    w_first = noise(part_keys[5], (MEMBERS, D, H), D ** -0.5, 0.15625, ((0, 8),))
    b_first = noise(part_keys[6], (MEMBERS, H), 0.5, 3.0, ((0, 8),))
    w_value = noise(part_keys[7], (MEMBERS, H), H ** -0.5, 0.1875, ((0, 8),))
    return dict(states=states, rewards=rewards, offsets=offsets, blocks=blocks, counts=counts, w_first=w_first, b_first=b_first, w_value=w_value)


discount = 0.8


def silu_slope(pre):
    sigma = jax.nn.sigmoid(pre)
    return sigma * (1.0 + pre * (1.0 - sigma))


def rounded(value):
    return lax.optimization_barrier(value.astype(jnp.bfloat16)).astype(jnp.float32)


def reference(states, rewards, offsets, blocks, counts, w_first, b_first, w_value):
    halves = N_REPLICA
    runs = ROLL_DEV // PEER_ROWS
    state_five = states.reshape(MEMBERS, halves, runs, PEER_ROWS, D)
    reward_four = rewards.reshape(MEMBERS, halves, runs, PEER_ROWS)
    offset_four = offsets.reshape(MEMBERS, halves, runs, PEER_ROWS)
    block_three = blocks.reshape(MEMBERS, halves, MEMBERS)
    source_idx = jnp.arange(MEMBERS, dtype=jnp.int32)[:, None]
    half_idx = jnp.arange(halves, dtype=jnp.int32)[None, :]
    position = jnp.arange(PEER_ROWS, dtype=jnp.int32)

    def one_member(member):
        picks = jnp.take(block_three, member, axis=2)
        features = jnp.transpose(state_five[source_idx, half_idx, picks], (1, 0, 2, 3))
        reward_rows = jnp.transpose(reward_four[source_idx, half_idx, picks], (1, 0, 2)).reshape(-1, PEER_ROWS)
        offset_rows = jnp.transpose(offset_four[source_idx, half_idx, picks], (1, 0, 2)).reshape(-1, PEER_ROWS)
        weight_one = w_first[member]
        bias_one = b_first[member].astype(jnp.float32)
        head = w_value[member].astype(jnp.float32)
        flat = features.reshape(-1, D)
        pre = jnp.dot(flat, weight_one, preferred_element_type=jnp.float32) + bias_one
        hidden = jax.nn.silu(pre)
        value = jnp.sum(hidden * head, axis=1).reshape(-1, PEER_ROWS)
        succ = jnp.minimum(position[None, :] + offset_rows, PEER_ROWS - 1)
        nexts = jnp.take_along_axis(value, succ, axis=1)
        factor = jnp.power(jnp.float32(discount), (succ - position[None, :]).astype(jnp.float32))
        delta = (reward_rows + factor * nexts - value).reshape(-1)
        order = jnp.arange(BATCH, dtype=jnp.int32)
        mask = (order < counts[member]).astype(jnp.float32)
        error = delta * mask
        dpre = (-error)[:, None] * head[None, :] * silu_slope(pre)
        dpre_low = dpre.astype(jnp.bfloat16)
        per_half = MEMBERS * PEER_ROWS
        total_w1 = jnp.zeros((D, H), jnp.float32)
        total_b1 = jnp.zeros((H,), jnp.float32)
        total_w2 = jnp.zeros((H,), jnp.float32)
        for half in range(halves):
            lower = half * per_half
            part_rows = flat[lower:lower + per_half]
            part_dpre = dpre_low[lower:lower + per_half]
            part_w1 = lax.dot_general(part_rows, part_dpre, (((0,), (0,)), ((), ())), preferred_element_type=jnp.float32)
            part_b1 = jnp.sum(dpre[lower:lower + per_half], axis=0)
            part_w2 = jnp.sum((-error[lower:lower + per_half])[:, None] * hidden[lower:lower + per_half], axis=0)
            total_w1 = total_w1 + rounded(part_w1)
            total_b1 = total_b1 + rounded(part_b1)
            total_w2 = total_w2 + rounded(part_w2)
        back = jnp.transpose(error.reshape(halves, MEMBERS, PEER_ROWS), (1, 0, 2)).reshape(SHARDS, PEER_ROWS)
        return total_w1.astype(jnp.bfloat16), total_b1, total_w2, back

    grad_w1, grad_b1, grad_w2, errors = lax.map(one_member, jnp.arange(MEMBERS, dtype=jnp.int32))
    return grad_w1, grad_b1, grad_w2, jnp.transpose(errors, (1, 0, 2))
```

```python
import functools
import math

import jax
import jax.numpy as jnp
from jax import lax
from jax.experimental import pallas as pl
from jax.experimental.pallas import tpu as pltpu
from jax.sharding import PartitionSpec as P

PEER_ROWS = 64
LANES = 128
CHUNK = 256
GROUP = 4 * PEER_ROWS

discount = 0.8


def partner(me, step, n):
    out = jnp.int32(0)
    bit = 1
    while bit < n:
        a = lax.rem(lax.div(me, jnp.int32(bit)), jnp.int32(2))
        b = lax.rem(lax.div(jnp.int32(step), jnp.int32(bit)), jnp.int32(2))
        out = out + (a + b - 2 * a * b) * bit
        bit *= 2
    return out


def kernel(
    n,
    blocks, counts, rewards, offsets, bias, head, states_hbm, w_hbm,
    grad_hbm, grad_b1, grad_w2, td,
    states, w, send, feats, aux_send, aux, err_send, err_recv,
    hid, slo, dpre, errs, acc, out_buf, b1_acc, w2_acc,
    local_sem, x_send, x_recv, f_send, f_recv, a_send, a_recv, g_send, g_recv, e_send, e_recv, out_sem,
):
    me = lax.axis_index("member")
    rep = lax.axis_index("replica")
    width = states_hbm.shape[2]
    hidden_units = w_hbm.shape[1]
    groups = n // 2

    load_states = pltpu.make_async_copy(states_hbm, states, local_sem.at[0])
    load_states.start()
    load_w = pltpu.make_async_copy(w_hbm, w, local_sem.at[1])
    load_w.start()

    barrier = pltpu.get_barrier_semaphore()

    def greet(step, carry):
        pl.semaphore_signal(
            barrier, inc=1, device_id={"member": partner(me, step, n)}, device_id_type=pl.DeviceIdType.MESH
        )
        return carry

    lax.fori_loop(1, n, greet, 0)
    pl.semaphore_signal(barrier, inc=1, device_id={"replica": 1 - rep}, device_id_type=pl.DeviceIdType.MESH)

    def rows_of(slot):
        return pl.ds(pl.multiple_of(slot * PEER_ROWS, PEER_ROWS), PEER_ROWS)

    def x_copy(step):
        return pltpu.make_async_remote_copy(
            src_ref=send.at[rows_of(step)], dst_ref=feats.at[rows_of(2 * step + rep)],
            send_sem=x_send.at[step], recv_sem=x_recv.at[step],
            device_id={"member": partner(me, step, n)}, device_id_type=pl.DeviceIdType.MESH,
        )

    def a_copy(step):
        return pltpu.make_async_remote_copy(
            src_ref=aux_send.at[step], dst_ref=aux.at[2 * step + rep],
            send_sem=a_send.at[step], recv_sem=a_recv.at[step],
            device_id={"member": partner(me, step, n)}, device_id_type=pl.DeviceIdType.MESH,
        )

    def f_copy(step):
        return pltpu.make_async_remote_copy(
            src_ref=feats.at[rows_of(2 * step + rep)], dst_ref=feats.at[rows_of(2 * step + rep)],
            send_sem=f_send.at[step], recv_sem=f_recv.at[step],
            device_id={"replica": 1 - rep}, device_id_type=pl.DeviceIdType.MESH,
        )

    def g_copy(step):
        return pltpu.make_async_remote_copy(
            src_ref=aux.at[2 * step + rep], dst_ref=aux.at[2 * step + rep],
            send_sem=g_send.at[step], recv_sem=g_recv.at[step],
            device_id={"replica": 1 - rep}, device_id_type=pl.DeviceIdType.MESH,
        )

    def e_copy(step, to, slot):
        return pltpu.make_async_remote_copy(
            src_ref=err_send.at[step], dst_ref=err_recv.at[slot],
            send_sem=e_send.at[step], recv_sem=e_recv.at[step],
            device_id={"member": to}, device_id_type=pl.DeviceIdType.MESH,
        )

    def picked_aux(run):
        half = lax.rem(run, jnp.int32(2))
        r = rewards[pl.ds(lax.div(run, jnp.int32(2)), 1), :]
        o = offsets[pl.ds(lax.div(run, jnp.int32(2)), 1), :].astype(jnp.float32)
        odd = jnp.full((1, LANES), half, jnp.int32) == 1
        r_other = pltpu.roll(r, PEER_ROWS, 1)
        o_other = pltpu.roll(o, PEER_ROWS, 1)
        lane = lax.broadcasted_iota(jnp.int32, (1, LANES), 1)
        row = jnp.where(
            lane < PEER_ROWS, jnp.where(odd, r_other, r), jnp.where(odd, o, o_other)
        )
        return jnp.broadcast_to(row, (8, LANES))

    def gather_aux(step, carry):
        run = blocks[0, partner(me, step, n)]
        aux_send[step] = picked_aux(run)
        return carry

    lax.fori_loop(1, n, gather_aux, 0)
    aux[rep] = picked_aux(blocks[0, me])
    load_states.wait()

    def gather(step, carry):
        run = blocks[0, partner(me, step, n)]
        send[rows_of(step), :] = states[run]
        return carry

    lax.fori_loop(1, n, gather, 0)
    feats[rows_of(rep), :] = states[blocks[0, me]]

    pl.semaphore_wait(barrier, n)

    def far_first(i, carry):
        step = lax.rem(i + n // 2, jnp.int32(n))
        x_copy(step).start()
        a_copy(step).start()
        return carry

    lax.fori_loop(0, n // 2, far_first, 0)
    f_copy(0).start()
    g_copy(0).start()
    lax.fori_loop(n // 2 + 1, n, far_first, 0)

    b1_acc[...] = jnp.zeros_like(b1_acc)
    w2_acc[...] = jnp.zeros_like(w2_acc)
    acc[...] = jnp.zeros_like(acc)
    load_w.wait()

    def head_group(g):
        for i in range(2):
            step = 2 * g + i

            def arrive():
                x_copy(step).wait_recv()
                f_copy(step).start()
                a_copy(step).wait_recv()
                g_copy(step).start()

            if i == 0:
                pl.when(g > 0)(arrive)
            else:
                arrive()
        for i in range(2):
            f_copy(2 * g + i).wait_recv()
            g_copy(2 * g + i).wait_recv()
        base = pl.multiple_of(g * GROUP, GROUP)
        x = feats[pl.ds(base, GROUP), :]
        total = jnp.zeros((GROUP, LANES), jnp.float32)
        for c in range(hidden_units // CHUNK):
            cols = slice(c * CHUNK, (c + 1) * CHUNK)
            pre = jnp.dot(x, w[:, cols], preferred_element_type=jnp.float32)
            pre = pre + bias[:, cols].astype(jnp.float32)
            hd = head[:, cols].astype(jnp.float32)
            sig = jax.nn.sigmoid(pre)
            h = pre * sig
            hid[:, cols] = h
            slo[:, cols] = (sig + h * (1.0 - sig)) * hd
            hv = h * hd
            for t in range(CHUNK // LANES):
                total = total + hv[:, t * LANES:(t + 1) * LANES]
        value = jnp.sum(total, axis=1, keepdims=True)
        row = lax.broadcasted_iota(jnp.int32, (PEER_ROWS, LANES), 0)
        lane = lax.broadcasted_iota(jnp.int32, (PEER_ROWS, LANES), 1)
        eye = lane == row
        count = counts[0]
        for i in range(4):
            step = 2 * g + i // 2
            half = i % 2
            a = jnp.broadcast_to(aux[4 * g + i][0:1, :], (PEER_ROWS, LANES))
            v = value[i * PEER_ROWS:(i + 1) * PEER_ROWS]
            v_row = jnp.sum(jnp.where(eye, v, 0.0), axis=0, keepdims=True)
            r_col = jnp.sum(jnp.where(eye, a, 0.0), axis=1, keepdims=True)
            o_col = jnp.sum(jnp.where(lane == row + PEER_ROWS, a, 0.0), axis=1, keepdims=True)
            succ = jnp.minimum(row.astype(jnp.float32) + o_col, PEER_ROWS - 1.0)
            nxt = jnp.sum(jnp.where(lane.astype(jnp.float32) == succ, v_row, 0.0), axis=1, keepdims=True)
            factor = jnp.exp2((succ - row.astype(jnp.float32)) * math.log2(discount))
            delta = r_col + factor * nxt - v
            q = (half * n + partner(me, step, n)) * PEER_ROWS + row
            err = jnp.where(q < count, delta, 0.0)
            errs[i * PEER_ROWS:(i + 1) * PEER_ROWS, :] = err
            e_row = jnp.sum(jnp.where(eye, err, 0.0), axis=0, keepdims=True)

            def give():
                err_send[step] = jnp.broadcast_to(e_row, (8, LANES))

            pl.when(rep == half)(give)
        for i in range(2):
            step = 2 * g + i

            def start_err():
                e_copy(step, partner(me, step, n), me).start()

            if i == 0:
                pl.when(g > 0)(start_err)
            else:
                start_err()
        for t in range(hidden_units // LANES):
            cols = slice(t * LANES, (t + 1) * LANES)
            neg = -errs[...]
            dp = neg * slo[:, cols]
            dpre[:, cols] = dp.astype(jnp.bfloat16)
            b1_acc[:, cols] += jnp.sum(dp.reshape(GROUP // 8, 8, LANES), axis=0)
            gw = neg * hid[:, cols]
            w2_acc[:, cols] += jnp.sum(gw.reshape(GROUP // 8, 8, LANES), axis=0)

    def grad_chunk(g, k):
        base = pl.multiple_of(g * GROUP, GROUP)
        cols = pl.ds(pl.multiple_of(k * CHUNK, CHUNK), CHUNK)
        return lax.dot_general(
            feats[pl.ds(base, GROUP), cols], dpre[...],
            (((0,), (0,)), ((), ())), preferred_element_type=jnp.float32,
        )

    def out_rows(k):
        return pl.ds(pl.multiple_of(k * CHUNK, CHUNK), CHUNK)

    def middle(g, carry):
        head_group(g)

        def add(k, c):
            acc[out_rows(k), :] += grad_chunk(g, k)
            return c

        lax.fori_loop(0, width // CHUNK, add, 0)
        return carry

    lax.fori_loop(0, groups - 1, middle, 0)
    last = jnp.int32(groups - 1)
    head_group(last)

    def out_copy(k):
        return pltpu.make_async_copy(out_buf.at[out_rows(k)], grad_hbm.at[out_rows(k)], out_sem.at[k])

    def finish(k, c):
        out_buf[out_rows(k), :] = (acc[out_rows(k), :] + grad_chunk(last, k)).astype(jnp.bfloat16)
        out_copy(k).start()
        return c

    lax.fori_loop(0, width // CHUNK, finish, 0)
    grad_b1[...] = jnp.sum(b1_acc[...], axis=0, keepdims=True)
    grad_w2[...] = jnp.sum(w2_acc[...], axis=0, keepdims=True)

    def drain(step, carry):
        x_copy(step).wait_send()
        a_copy(step).wait_send()
        e_copy(step, partner(me, step, n), me).wait()
        return carry

    lax.fori_loop(1, n, drain, 0)

    def drain_forward(step, carry):
        f_copy(step).wait_send()
        g_copy(step).wait_send()
        return carry

    lax.fori_loop(0, n, drain_forward, 0)
    err_recv[me] = err_send[0]
    for m in range(n):
        td[m:m + 1, :] = err_recv[m][0:1, :PEER_ROWS]

    def finish_out(k, c):
        out_copy(k).wait()
        return c

    lax.fori_loop(0, width // CHUNK, finish_out, 0)


def per_device(states, rewards, offsets, blocks, counts, w_first, b_first, w_value):
    n = lax.axis_size("member")
    rows, width = states.shape
    units = w_first.shape[2]
    runs = rows // PEER_ROWS
    vmem = pl.BlockSpec(memory_space=pltpu.VMEM)
    smem = pl.BlockSpec(memory_space=pltpu.SMEM)
    hbm = pl.BlockSpec(memory_space=pl.ANY)
    f32, bf16 = jnp.float32, jnp.bfloat16
    dma = pltpu.SemaphoreType.DMA
    grad, b1, w2, td = pl.pallas_call(
        functools.partial(kernel, n),
        out_shape=(
            jax.ShapeDtypeStruct((width, units), bf16),
            jax.ShapeDtypeStruct((1, units), f32),
            jax.ShapeDtypeStruct((1, units), f32),
            jax.ShapeDtypeStruct((n, PEER_ROWS), f32),
        ),
        in_specs=[smem, smem, vmem, vmem, vmem, vmem, hbm, hbm],
        out_specs=(hbm, vmem, vmem, vmem),
        scratch_shapes=[
            pltpu.VMEM((runs, PEER_ROWS, width), bf16),
            pltpu.VMEM((width, units), bf16),
            pltpu.VMEM((n * PEER_ROWS, width), bf16),
            pltpu.VMEM((2 * n * PEER_ROWS, width), bf16),
            pltpu.VMEM((n, 8, LANES), f32),
            pltpu.VMEM((2 * n, 8, LANES), f32),
            pltpu.VMEM((n, 8, LANES), f32),
            pltpu.VMEM((n, 8, LANES), f32),
            pltpu.VMEM((GROUP, units), f32),
            pltpu.VMEM((GROUP, units), f32),
            pltpu.VMEM((GROUP, units), bf16),
            pltpu.VMEM((GROUP, LANES), f32),
            pltpu.VMEM((width, units), f32),
            pltpu.VMEM((width, units), bf16),
            pltpu.VMEM((8, units), f32),
            pltpu.VMEM((8, units), f32),
            dma((2,)),
            dma((n,)), dma((n,)), dma((n,)), dma((n,)), dma((n,)), dma((n,)),
            dma((n,)), dma((n,)), dma((n,)), dma((n,)),
            dma((width // CHUNK,)),
        ],
        compiler_params=pltpu.CompilerParams(
            collective_id=0, has_side_effects=True, vmem_limit_bytes=56 * 1024 * 1024,
        ),
        cost_estimate=pl.CostEstimate(
            flops=8 * n * PEER_ROWS * width * units,
            bytes_accessed=2 * (rows * width + 2 * width * units),
            transcendentals=2 * n * PEER_ROWS * units,
        ),
    )(
        blocks, counts, rewards.reshape(-1, LANES), offsets.reshape(-1, LANES),
        b_first, w_value, states.reshape(runs, PEER_ROWS, width), w_first[0],
    )
    return grad[None], b1, w2, td[None]


def solution(mesh):
    placed = (
        P(("groups", "member", "replica"), None),
        P(("groups", "member", "replica")),
        P(("groups", "member", "replica")),
        P(("groups", "member", "replica"), None),
        P(("groups", "member")),
        P(("groups", "member"), None, None),
        P(("groups", "member"), None),
        P(("groups", "member"), None),
    )
    return jax.shard_map(
        per_device,
        mesh=mesh,
        in_specs=placed,
        out_specs=(
            P(("groups", "member"), None, None),
            P(("groups", "member"), None),
            P(("groups", "member"), None),
            P(("groups", "member", "replica"), None, None),
        ),
        check_vma=False,
    )
```

```python
import functools
import math

import jax
import jax.numpy as jnp
from jax import lax
from jax.experimental import pallas as pl
from jax.experimental.pallas import tpu as pltpu
from jax.sharding import PartitionSpec as P

PEER_ROWS = 64
LANES = 128
CHUNK = 256
GROUP = 4 * PEER_ROWS

discount = 0.8


def partner(me, step, n):
    out = jnp.int32(0)
    bit = 1
    while bit < n:
        a = lax.rem(lax.div(me, jnp.int32(bit)), jnp.int32(2))
        b = lax.rem(lax.div(jnp.int32(step), jnp.int32(bit)), jnp.int32(2))
        out = out + (a + b - 2 * a * b) * bit
        bit *= 2
    return out


def kernel(
    n,
    blocks, counts, rewards, offsets, bias, head, states_hbm, w_hbm,
    acc, last_feats, dpre, b1_acc, w2_acc, td,
    states, w, send, feats, aux_send, aux, err_send, err_recv,
    hid, slo, errs,
    local_sem, x_send, x_recv, f_send, f_recv, a_send, a_recv, g_send, g_recv, e_send, e_recv,
):
    me = lax.axis_index("member")
    rep = lax.axis_index("replica")
    width = states_hbm.shape[2]
    hidden_units = w_hbm.shape[1]
    groups = n // 2

    load_states = pltpu.make_async_copy(states_hbm, states, local_sem.at[0])
    load_states.start()
    load_w = pltpu.make_async_copy(w_hbm, w, local_sem.at[1])
    load_w.start()

    barrier = pltpu.get_barrier_semaphore()

    def greet(step, carry):
        pl.semaphore_signal(
            barrier, inc=1, device_id={"member": partner(me, step, n)}, device_id_type=pl.DeviceIdType.MESH
        )
        return carry

    lax.fori_loop(1, n, greet, 0)
    pl.semaphore_signal(barrier, inc=1, device_id={"replica": 1 - rep}, device_id_type=pl.DeviceIdType.MESH)

    def rows_of(slot):
        return pl.ds(pl.multiple_of(slot * PEER_ROWS, PEER_ROWS), PEER_ROWS)

    def x_copy(step):
        return pltpu.make_async_remote_copy(
            src_ref=send.at[rows_of(step)], dst_ref=feats.at[rows_of(2 * step + rep)],
            send_sem=x_send.at[step], recv_sem=x_recv.at[step],
            device_id={"member": partner(me, step, n)}, device_id_type=pl.DeviceIdType.MESH,
        )

    def a_copy(step):
        return pltpu.make_async_remote_copy(
            src_ref=aux_send.at[step], dst_ref=aux.at[2 * step + rep],
            send_sem=a_send.at[step], recv_sem=a_recv.at[step],
            device_id={"member": partner(me, step, n)}, device_id_type=pl.DeviceIdType.MESH,
        )

    def f_copy(step):
        return pltpu.make_async_remote_copy(
            src_ref=feats.at[rows_of(2 * step + rep)], dst_ref=feats.at[rows_of(2 * step + rep)],
            send_sem=f_send.at[step], recv_sem=f_recv.at[step],
            device_id={"replica": 1 - rep}, device_id_type=pl.DeviceIdType.MESH,
        )

    def g_copy(step):
        return pltpu.make_async_remote_copy(
            src_ref=aux.at[2 * step + rep], dst_ref=aux.at[2 * step + rep],
            send_sem=g_send.at[step], recv_sem=g_recv.at[step],
            device_id={"replica": 1 - rep}, device_id_type=pl.DeviceIdType.MESH,
        )

    def e_copy(step, to, slot):
        return pltpu.make_async_remote_copy(
            src_ref=err_send.at[step], dst_ref=err_recv.at[slot],
            send_sem=e_send.at[step], recv_sem=e_recv.at[step],
            device_id={"member": to}, device_id_type=pl.DeviceIdType.MESH,
        )

    def picked_aux(run):
        half = lax.rem(run, jnp.int32(2))
        r = rewards[pl.ds(lax.div(run, jnp.int32(2)), 1), :]
        o = offsets[pl.ds(lax.div(run, jnp.int32(2)), 1), :].astype(jnp.float32)
        odd = jnp.full((1, LANES), half, jnp.int32) == 1
        r_other = pltpu.roll(r, PEER_ROWS, 1)
        o_other = pltpu.roll(o, PEER_ROWS, 1)
        lane = lax.broadcasted_iota(jnp.int32, (1, LANES), 1)
        row = jnp.where(
            lane < PEER_ROWS, jnp.where(odd, r_other, r), jnp.where(odd, o, o_other)
        )
        return jnp.broadcast_to(row, (8, LANES))

    def gather_aux(step, carry):
        run = blocks[0, partner(me, step, n)]
        aux_send[step] = picked_aux(run)
        return carry

    lax.fori_loop(1, n, gather_aux, 0)
    aux[rep] = picked_aux(blocks[0, me])
    load_states.wait()

    def gather(step, carry):
        run = blocks[0, partner(me, step, n)]
        send[rows_of(step), :] = states[run]
        return carry

    lax.fori_loop(1, n, gather, 0)
    feats[rows_of(rep), :] = states[blocks[0, me]]

    pl.semaphore_wait(barrier, n)

    def far_first(i, carry):
        step = lax.rem(i + n // 2, jnp.int32(n))
        x_copy(step).start()
        return carry

    def aux_first(step, carry):
        a_copy(step).start()
        return carry

    lax.fori_loop(1, n, aux_first, 0)
    lax.fori_loop(0, n // 2, far_first, 0)
    f_copy(0).start()
    g_copy(0).start()
    lax.fori_loop(n // 2 + 1, n, far_first, 0)

    b1_acc[...] = jnp.zeros_like(b1_acc)
    w2_acc[...] = jnp.zeros_like(w2_acc)
    acc[...] = jnp.zeros_like(acc)
    load_w.wait()

    def aux_forward(step, carry):
        a_copy(step).wait_recv()
        g_copy(step).start()
        return carry

    def aux_arrive(step, carry):
        g_copy(step).wait_recv()
        return carry

    lax.fori_loop(1, n, aux_forward, 0)
    lax.fori_loop(0, n, aux_arrive, 0)

    def head_group(g):
        for i in range(2):
            step = 2 * g + i

            def arrive():
                x_copy(step).wait_recv()
                f_copy(step).start()

            if i == 0:
                pl.when(g > 0)(arrive)
            else:
                arrive()
        for i in range(2):
            f_copy(2 * g + i).wait_recv()
        base = pl.multiple_of(g * GROUP, GROUP)
        x = feats[pl.ds(base, GROUP), :]
        total = jnp.zeros((GROUP, LANES), jnp.float32)
        for c in range(hidden_units // CHUNK):
            cols = slice(c * CHUNK, (c + 1) * CHUNK)
            pre = jnp.dot(x, w[:, cols], preferred_element_type=jnp.float32)
            pre = pre + bias[:, cols].astype(jnp.float32)
            hd = head[:, cols].astype(jnp.float32)
            sig = 0.5 * jnp.tanh(0.5 * pre) + 0.5
            h = pre * sig
            hid[:, cols] = h
            slo[:, cols] = (sig + h * (1.0 - sig)) * hd
            hv = h * hd
            for t in range(CHUNK // LANES):
                total = total + hv[:, t * LANES:(t + 1) * LANES]
        value = jnp.sum(total, axis=1, keepdims=True)
        row = lax.broadcasted_iota(jnp.int32, (PEER_ROWS, LANES), 0)
        lane = lax.broadcasted_iota(jnp.int32, (PEER_ROWS, LANES), 1)
        eye = lane == row
        count = counts[0]
        e_rows = []
        for i in range(4):
            step = 2 * g + i // 2
            half = i % 2
            a = jnp.broadcast_to(aux[4 * g + i][0:1, :], (PEER_ROWS, LANES))
            v = value[i * PEER_ROWS:(i + 1) * PEER_ROWS]
            v_row = jnp.sum(jnp.where(eye, v, 0.0), axis=0, keepdims=True)
            r_col = jnp.sum(jnp.where(eye, a, 0.0), axis=1, keepdims=True)
            o_col = jnp.sum(jnp.where(lane == row + PEER_ROWS, a, 0.0), axis=1, keepdims=True)
            succ = jnp.minimum(row.astype(jnp.float32) + o_col, PEER_ROWS - 1.0)
            nxt = jnp.sum(jnp.where(lane.astype(jnp.float32) == succ, v_row, 0.0), axis=1, keepdims=True)
            factor = jnp.exp2((succ - row.astype(jnp.float32)) * math.log2(discount))
            delta = r_col + factor * nxt - v
            q = (half * n + partner(me, step, n)) * PEER_ROWS + row
            err = jnp.where(q < count, delta, 0.0)
            errs[i * PEER_ROWS:(i + 1) * PEER_ROWS, :] = err
            e_rows.append(jnp.sum(jnp.where(eye, err, 0.0), axis=0, keepdims=True))
        mine = jnp.full((8, LANES), rep, jnp.int32) == 0
        for i in range(2):
            err_send[2 * g + i] = jnp.where(mine, e_rows[2 * i], e_rows[2 * i + 1])
        for i in range(2):
            step = 2 * g + i

            def start_err():
                e_copy(step, partner(me, step, n), me).start()

            if i == 0:
                pl.when(g > 0)(start_err)
            else:
                start_err()
        for t in range(hidden_units // LANES):
            cols = slice(t * LANES, (t + 1) * LANES)
            neg = -errs[...]
            dp = neg * slo[:, cols]
            dpre[:, cols] = dp.astype(jnp.bfloat16)
            b1_acc[:, cols] += jnp.sum(dp.reshape(GROUP // 8, 8, LANES), axis=0)
            gw = neg * hid[:, cols]
            w2_acc[:, cols] += jnp.sum(gw.reshape(GROUP // 8, 8, LANES), axis=0)

    def grad_chunk(g, k):
        base = pl.multiple_of(g * GROUP, GROUP)
        cols = pl.ds(pl.multiple_of(k * CHUNK, CHUNK), CHUNK)
        return lax.dot_general(
            feats[pl.ds(base, GROUP), cols], dpre[...],
            (((0,), (0,)), ((), ())), preferred_element_type=jnp.float32,
        )

    def out_rows(k):
        return pl.ds(pl.multiple_of(k * CHUNK, CHUNK), CHUNK)

    def middle(g, carry):
        head_group(g)

        def add(k, c):
            acc[out_rows(k), :] += grad_chunk(g, k)
            return c

        lax.fori_loop(0, width // CHUNK, add, 0)
        return carry

    lax.fori_loop(0, groups - 1, middle, 0)
    last = jnp.int32(groups - 1)
    head_group(last)

    last_feats[...] = feats[pl.ds((groups - 1) * GROUP, GROUP), :]

    def drain(step, carry):
        x_copy(step).wait_send()
        a_copy(step).wait_send()
        e_copy(step, partner(me, step, n), me).wait()
        return carry

    lax.fori_loop(1, n, drain, 0)

    def drain_forward(step, carry):
        f_copy(step).wait_send()
        g_copy(step).wait_send()
        return carry

    lax.fori_loop(0, n, drain_forward, 0)
    err_recv[me] = err_send[0]
    for m in range(n):
        td[m:m + 1, :] = err_recv[m][0:1, :PEER_ROWS]


def final_kernel(acc, feats, dpre, b1_acc, w2_acc, td_in, grad_hbm, grad_b1, grad_w2, td, out_buf, out_sem):
    def rows(k):
        return pl.ds(pl.multiple_of(k * CHUNK, CHUNK), CHUNK)

    def out_copy(k):
        return pltpu.make_async_copy(out_buf.at[rows(k)], grad_hbm.at[rows(k)], out_sem.at[k])

    steps = acc.shape[0] // CHUNK

    def finish(k, c):
        part = lax.dot_general(
            feats[:, rows(k)], dpre[...], (((0,), (0,)), ((), ())), preferred_element_type=jnp.float32
        )
        out_buf[rows(k), :] = (acc[rows(k), :] + part).astype(jnp.bfloat16)
        out_copy(k).start()
        return c

    lax.fori_loop(0, steps, finish, 0)
    grad_b1[...] = jnp.sum(b1_acc[...], axis=0, keepdims=True)
    grad_w2[...] = jnp.sum(w2_acc[...], axis=0, keepdims=True)
    td[...] = td_in[...]

    def finish_out(k, c):
        out_copy(k).wait()
        return c

    lax.fori_loop(0, steps, finish_out, 0)


def per_device(states, rewards, offsets, blocks, counts, w_first, b_first, w_value):
    n = lax.axis_size("member")
    rows, width = states.shape
    units = w_first.shape[2]
    runs = rows // PEER_ROWS
    vmem = pl.BlockSpec(memory_space=pltpu.VMEM)
    smem = pl.BlockSpec(memory_space=pltpu.SMEM)
    hbm = pl.BlockSpec(memory_space=pltpu.HBM)
    f32, bf16 = jnp.float32, jnp.bfloat16
    dma = pltpu.SemaphoreType.DMA
    limit = 55 * 2**20
    held = pl.pallas_call(
        functools.partial(kernel, n),
        out_shape=(
            pltpu.VMEM((width, units), f32),
            pltpu.VMEM((GROUP, width), bf16),
            pltpu.VMEM((GROUP, units), bf16),
            pltpu.VMEM((8, units), f32),
            pltpu.VMEM((8, units), f32),
            pltpu.VMEM((n, PEER_ROWS), f32),
        ),
        in_specs=[smem, smem, vmem, vmem, vmem, vmem, hbm, hbm],
        out_specs=(vmem,) * 6,
        scratch_shapes=[
            pltpu.VMEM((runs, PEER_ROWS, width), bf16),
            pltpu.VMEM((width, units), bf16),
            pltpu.VMEM((n * PEER_ROWS, width), bf16),
            pltpu.VMEM((2 * n * PEER_ROWS, width), bf16),
            pltpu.VMEM((n, 8, LANES), f32),
            pltpu.VMEM((2 * n, 8, LANES), f32),
            pltpu.VMEM((n, 8, LANES), f32),
            pltpu.VMEM((n, 8, LANES), f32),
            pltpu.VMEM((GROUP, units), f32),
            pltpu.VMEM((GROUP, units), f32),
            pltpu.VMEM((GROUP, LANES), f32),
            dma((2,)),
            dma((n,)), dma((n,)), dma((n,)), dma((n,)), dma((n,)), dma((n,)),
            dma((n,)), dma((n,)), dma((n,)), dma((n,)),
        ],
        compiler_params=pltpu.CompilerParams(
            collective_id=0, has_side_effects=True, vmem_limit_bytes=limit,
        ),
        cost_estimate=pl.CostEstimate(
            flops=8 * n * PEER_ROWS * width * units,
            bytes_accessed=2 * (rows * width + 2 * width * units),
            transcendentals=2 * n * PEER_ROWS * units,
        ),
    )(
        blocks, counts, rewards.reshape(-1, LANES), offsets.reshape(-1, LANES),
        b_first, w_value, states.reshape(runs, PEER_ROWS, width), w_first[0],
    )
    grad, b1, w2, td = pl.pallas_call(
        final_kernel,
        out_shape=(
            jax.ShapeDtypeStruct((width, units), bf16),
            jax.ShapeDtypeStruct((1, units), f32),
            jax.ShapeDtypeStruct((1, units), f32),
            jax.ShapeDtypeStruct((n, PEER_ROWS), f32),
        ),
        in_specs=[vmem] * 6,
        out_specs=(hbm, vmem, vmem, vmem),
        scratch_shapes=[pltpu.VMEM((width, units), bf16), dma((width // CHUNK,))],
        compiler_params=pltpu.CompilerParams(vmem_limit_bytes=24 * 1024 * 1024),
        cost_estimate=pl.CostEstimate(
            flops=2 * GROUP * width * units, bytes_accessed=2 * width * units, transcendentals=0
        ),
    )(*held)
    return grad[None], b1, w2, td[None]


def solution(mesh):
    placed = (
        P(("groups", "member", "replica"), None),
        P(("groups", "member", "replica")),
        P(("groups", "member", "replica")),
        P(("groups", "member", "replica"), None),
        P(("groups", "member")),
        P(("groups", "member"), None, None),
        P(("groups", "member"), None),
        P(("groups", "member"), None),
    )
    return jax.shard_map(
        per_device,
        mesh=mesh,
        in_specs=placed,
        out_specs=(
            P(("groups", "member"), None, None),
            P(("groups", "member"), None),
            P(("groups", "member"), None),
            P(("groups", "member", "replica"), None, None),
        ),
        check_vma=False,
    )
```

```python
import functools
import math

import jax
import jax.numpy as jnp
from jax import lax
from jax.experimental import pallas as pl
from jax.experimental.pallas import tpu as pltpu
from jax.sharding import PartitionSpec as P

PEER_ROWS = 64
LANES = 128
CHUNK = 256
GROUP = 4 * PEER_ROWS

discount = 0.8


def partner(me, step, n):
    out = jnp.int32(0)
    bit = 1
    while bit < n:
        a = lax.rem(lax.div(me, jnp.int32(bit)), jnp.int32(2))
        b = lax.rem(lax.div(jnp.int32(step), jnp.int32(bit)), jnp.int32(2))
        out = out + (a + b - 2 * a * b) * bit
        bit *= 2
    return out


def kernel(
    n,
    blocks, counts, rewards, offsets, bias, head, states_hbm, w_hbm,
    grad, b1_acc, w2_acc, td,
    states, w, send, feats, aux_send, aux, err_send, err_recv,
    hid, slo, errs, acc, dpre,
    local_sem, x_send, x_recv, f_send, f_recv, a_send, a_recv, g_send, g_recv, e_send, e_recv,
):
    me = lax.axis_index("member")
    rep = lax.axis_index("replica")
    width = states_hbm.shape[2]
    hidden_units = w_hbm.shape[1]
    groups = n // 2

    load_states = pltpu.make_async_copy(states_hbm, states, local_sem.at[0])
    load_states.start()
    load_w = pltpu.make_async_copy(w_hbm, w, local_sem.at[1])
    load_w.start()

    barrier = pltpu.get_barrier_semaphore()

    def greet(step, carry):
        pl.semaphore_signal(
            barrier, inc=1, device_id={"member": partner(me, step, n)}, device_id_type=pl.DeviceIdType.MESH
        )
        return carry

    lax.fori_loop(1, n, greet, 0)
    pl.semaphore_signal(barrier, inc=1, device_id={"replica": 1 - rep}, device_id_type=pl.DeviceIdType.MESH)

    def rows_of(slot):
        return pl.ds(pl.multiple_of(slot * PEER_ROWS, PEER_ROWS), PEER_ROWS)

    def x_copy(step):
        return pltpu.make_async_remote_copy(
            src_ref=send.at[rows_of(step)], dst_ref=feats.at[rows_of(2 * step + rep)],
            send_sem=x_send.at[step], recv_sem=x_recv.at[step],
            device_id={"member": partner(me, step, n)}, device_id_type=pl.DeviceIdType.MESH,
        )

    def a_copy(step):
        return pltpu.make_async_remote_copy(
            src_ref=aux_send.at[step], dst_ref=aux.at[2 * step + rep],
            send_sem=a_send.at[step], recv_sem=a_recv.at[step],
            device_id={"member": partner(me, step, n)}, device_id_type=pl.DeviceIdType.MESH,
        )

    def f_copy(step):
        return pltpu.make_async_remote_copy(
            src_ref=feats.at[rows_of(2 * step + rep)], dst_ref=feats.at[rows_of(2 * step + rep)],
            send_sem=f_send.at[step], recv_sem=f_recv.at[step],
            device_id={"replica": 1 - rep}, device_id_type=pl.DeviceIdType.MESH,
        )

    def g_copy(step):
        return pltpu.make_async_remote_copy(
            src_ref=aux.at[2 * step + rep], dst_ref=aux.at[2 * step + rep],
            send_sem=g_send.at[step], recv_sem=g_recv.at[step],
            device_id={"replica": 1 - rep}, device_id_type=pl.DeviceIdType.MESH,
        )

    def e_copy(step, to, slot):
        return pltpu.make_async_remote_copy(
            src_ref=err_send.at[step], dst_ref=err_recv.at[slot],
            send_sem=e_send.at[step], recv_sem=e_recv.at[step],
            device_id={"member": to}, device_id_type=pl.DeviceIdType.MESH,
        )

    def picked_aux(run):
        half = lax.rem(run, jnp.int32(2))
        r = rewards[pl.ds(lax.div(run, jnp.int32(2)), 1), :]
        o = offsets[pl.ds(lax.div(run, jnp.int32(2)), 1), :].astype(jnp.float32)
        odd = jnp.full((1, LANES), half, jnp.int32) == 1
        r_other = pltpu.roll(r, PEER_ROWS, 1)
        o_other = pltpu.roll(o, PEER_ROWS, 1)
        lane = lax.broadcasted_iota(jnp.int32, (1, LANES), 1)
        row = jnp.where(
            lane < PEER_ROWS, jnp.where(odd, r_other, r), jnp.where(odd, o, o_other)
        )
        return jnp.broadcast_to(row, (8, LANES))

    def gather_aux(step, carry):
        run = blocks[0, partner(me, step, n)]
        aux_send[step] = picked_aux(run)
        return carry

    lax.fori_loop(1, n, gather_aux, 0)
    aux[rep] = picked_aux(blocks[0, me])
    load_states.wait()

    def gather(step, carry):
        run = blocks[0, partner(me, step, n)]
        send[rows_of(step), :] = states[run]
        return carry

    lax.fori_loop(1, n, gather, 0)
    feats[rows_of(rep), :] = states[blocks[0, me]]

    pl.semaphore_wait(barrier, n)

    def far_first(i, carry):
        step = lax.rem(i + n // 2, jnp.int32(n))
        x_copy(step).start()
        return carry

    def aux_first(step, carry):
        a_copy(step).start()
        return carry

    lax.fori_loop(1, n, aux_first, 0)
    lax.fori_loop(0, n // 2, far_first, 0)
    f_copy(0).start()
    g_copy(0).start()
    lax.fori_loop(n // 2 + 1, n, far_first, 0)

    b1_acc[...] = jnp.zeros_like(b1_acc)
    w2_acc[...] = jnp.zeros_like(w2_acc)
    acc[...] = jnp.zeros_like(acc)
    load_w.wait()

    def aux_forward(step, carry):
        a_copy(step).wait_recv()
        g_copy(step).start()
        return carry

    def aux_arrive(step, carry):
        g_copy(step).wait_recv()
        return carry

    lax.fori_loop(1, n, aux_forward, 0)
    lax.fori_loop(0, n, aux_arrive, 0)

    def head_group(g, slot):
        for i in range(2):
            step = 2 * g + i

            def arrive():
                x_copy(step).wait_recv()
                f_copy(step).start()

            if i == 0:
                pl.when(g > 0)(arrive)
            else:
                arrive()
        for i in range(2):
            f_copy(2 * g + i).wait_recv()
        base = pl.multiple_of(g * GROUP, GROUP)
        x = feats[pl.ds(base, GROUP), :]
        total = jnp.zeros((GROUP, LANES), jnp.float32)
        for c in range(hidden_units // CHUNK):
            cols = slice(c * CHUNK, (c + 1) * CHUNK)
            pre = jnp.dot(x, w[:, cols], preferred_element_type=jnp.float32)
            pre = pre + bias[:, cols].astype(jnp.float32)
            hd = head[:, cols].astype(jnp.float32)
            sig = 0.5 * jnp.tanh(0.5 * pre) + 0.5
            h = pre * sig
            hid[:, cols] = h
            slo[:, cols] = (sig + h * (1.0 - sig)) * hd
            hv = h * hd
            for t in range(CHUNK // LANES):
                total = total + hv[:, t * LANES:(t + 1) * LANES]
        value = jnp.sum(total, axis=1, keepdims=True)
        row = lax.broadcasted_iota(jnp.int32, (PEER_ROWS, LANES), 0)
        lane = lax.broadcasted_iota(jnp.int32, (PEER_ROWS, LANES), 1)
        eye = lane == row
        count = counts[0]
        e_rows = []
        for i in range(4):
            step = 2 * g + i // 2
            half = i % 2
            a = jnp.broadcast_to(aux[4 * g + i][0:1, :], (PEER_ROWS, LANES))
            v = value[i * PEER_ROWS:(i + 1) * PEER_ROWS]
            v_row = jnp.sum(jnp.where(eye, v, 0.0), axis=0, keepdims=True)
            r_col = jnp.sum(jnp.where(eye, a, 0.0), axis=1, keepdims=True)
            o_col = jnp.sum(jnp.where(lane == row + PEER_ROWS, a, 0.0), axis=1, keepdims=True)
            succ = jnp.minimum(row.astype(jnp.float32) + o_col, PEER_ROWS - 1.0)
            nxt = jnp.sum(jnp.where(lane.astype(jnp.float32) == succ, v_row, 0.0), axis=1, keepdims=True)
            factor = jnp.exp2((succ - row.astype(jnp.float32)) * math.log2(discount))
            delta = r_col + factor * nxt - v
            q = (half * n + partner(me, step, n)) * PEER_ROWS + row
            err = jnp.where(q < count, delta, 0.0)
            errs[i * PEER_ROWS:(i + 1) * PEER_ROWS, :] = err
            e_rows.append(jnp.sum(jnp.where(eye, err, 0.0), axis=0, keepdims=True))
        mine = jnp.full((8, LANES), rep, jnp.int32) == 0
        for i in range(2):
            err_send[2 * g + i] = jnp.where(mine, e_rows[2 * i], e_rows[2 * i + 1])
        for i in range(2):
            step = 2 * g + i

            def start_err():
                e_copy(step, partner(me, step, n), me).start()

            if i == 0:
                pl.when(g > 0)(start_err)
            else:
                start_err()
        for t in range(hidden_units // LANES):
            cols = slice(t * LANES, (t + 1) * LANES)
            neg = -errs[...]
            dp = neg * slo[:, cols]
            dpre[slot * GROUP:(slot + 1) * GROUP, cols] = dp.astype(jnp.bfloat16)
            b1_acc[:, cols] += jnp.sum(dp.reshape(GROUP // 8, 8, LANES), axis=0)
            gw = neg * hid[:, cols]
            w2_acc[:, cols] += jnp.sum(gw.reshape(GROUP // 8, 8, LANES), axis=0)

    def grad_chunk(g, k, rows):
        base = pl.multiple_of(g * GROUP, GROUP)
        cols = pl.ds(pl.multiple_of(k * CHUNK, CHUNK), CHUNK)
        return lax.dot_general(
            feats[pl.ds(base, rows), cols], dpre[:rows, :],
            (((0,), (0,)), ((), ())), preferred_element_type=jnp.float32,
        )

    def out_rows(k):
        return pl.ds(pl.multiple_of(k * CHUNK, CHUNK), CHUNK)

    def middle(g, carry):
        head_group(g, 0)

        def add(k, c):
            acc[out_rows(k), :] += grad_chunk(g, k, GROUP)
            return c

        lax.fori_loop(0, width // CHUNK, add, 0)
        return carry

    lax.fori_loop(0, groups - 2, middle, 0)
    before = jnp.int32(groups - 2)
    head_group(before, 0)
    head_group(jnp.int32(groups - 1), 1)

    def finish(k, c):
        grad[out_rows(k), :] = (acc[out_rows(k), :] + grad_chunk(before, k, 2 * GROUP)).astype(jnp.bfloat16)
        return c

    lax.fori_loop(0, width // CHUNK, finish, 0)

    def drain(step, carry):
        x_copy(step).wait_send()
        a_copy(step).wait_send()
        e_copy(step, partner(me, step, n), me).wait()
        return carry

    lax.fori_loop(1, n, drain, 0)

    def drain_forward(step, carry):
        f_copy(step).wait_send()
        g_copy(step).wait_send()
        return carry

    lax.fori_loop(0, n, drain_forward, 0)
    err_recv[me] = err_send[0]
    for m in range(n):
        td[m:m + 1, :] = err_recv[m][0:1, :PEER_ROWS]


def final_kernel(grad, b1_acc, w2_acc, td_in, grad_hbm, grad_b1, grad_w2, td, out_sem):
    steps = grad.shape[0] // CHUNK

    def out_copy(k):
        rows = slice(k * CHUNK, (k + 1) * CHUNK)
        return pltpu.make_async_copy(grad.at[rows], grad_hbm.at[rows], out_sem.at[k])

    for k in range(steps):
        out_copy(k).start()
    grad_b1[...] = jnp.sum(b1_acc[...], axis=0, keepdims=True)
    grad_w2[...] = jnp.sum(w2_acc[...], axis=0, keepdims=True)
    td[...] = td_in[...]
    for k in range(steps):
        out_copy(k).wait()


def per_device(states, rewards, offsets, blocks, counts, w_first, b_first, w_value):
    n = lax.axis_size("member")
    rows, width = states.shape
    units = w_first.shape[2]
    runs = rows // PEER_ROWS
    vmem = pl.BlockSpec(memory_space=pltpu.VMEM)
    smem = pl.BlockSpec(memory_space=pltpu.SMEM)
    hbm = pl.BlockSpec(memory_space=pltpu.HBM)
    f32, bf16 = jnp.float32, jnp.bfloat16
    dma = pltpu.SemaphoreType.DMA
    limit = 60 * 2**20
    held = pl.pallas_call(
        functools.partial(kernel, n),
        out_shape=(
            pltpu.VMEM((width, units), bf16),
            pltpu.VMEM((8, units), f32),
            pltpu.VMEM((8, units), f32),
            pltpu.VMEM((n, PEER_ROWS), f32),
        ),
        in_specs=[smem, smem, vmem, vmem, vmem, vmem, hbm, hbm],
        out_specs=(vmem,) * 4,
        scratch_shapes=[
            pltpu.VMEM((runs, PEER_ROWS, width), bf16),
            pltpu.VMEM((width, units), bf16),
            pltpu.VMEM((n * PEER_ROWS, width), bf16),
            pltpu.VMEM((2 * n * PEER_ROWS, width), bf16),
            pltpu.VMEM((n, 8, LANES), f32),
            pltpu.VMEM((2 * n, 8, LANES), f32),
            pltpu.VMEM((n, 8, LANES), f32),
            pltpu.VMEM((n, 8, LANES), f32),
            pltpu.VMEM((GROUP, units), f32),
            pltpu.VMEM((GROUP, units), f32),
            pltpu.VMEM((GROUP, LANES), f32),
            pltpu.VMEM((width, units), f32),
            pltpu.VMEM((2 * GROUP, units), bf16),
            dma((2,)),
            dma((n,)), dma((n,)), dma((n,)), dma((n,)), dma((n,)), dma((n,)),
            dma((n,)), dma((n,)), dma((n,)), dma((n,)),
        ],
        compiler_params=pltpu.CompilerParams(
            collective_id=0, has_side_effects=True, vmem_limit_bytes=limit,
        ),
        cost_estimate=pl.CostEstimate(
            flops=8 * n * PEER_ROWS * width * units,
            bytes_accessed=2 * (rows * width + 2 * width * units),
            transcendentals=2 * n * PEER_ROWS * units,
        ),
    )(
        blocks, counts, rewards.reshape(-1, LANES), offsets.reshape(-1, LANES),
        b_first, w_value, states.reshape(runs, PEER_ROWS, width), w_first[0],
    )
    grad, b1, w2, td = pl.pallas_call(
        final_kernel,
        out_shape=(
            jax.ShapeDtypeStruct((width, units), bf16),
            jax.ShapeDtypeStruct((1, units), f32),
            jax.ShapeDtypeStruct((1, units), f32),
            jax.ShapeDtypeStruct((n, PEER_ROWS), f32),
        ),
        in_specs=[vmem] * 4,
        out_specs=(hbm, vmem, vmem, vmem),
        scratch_shapes=[dma((width // CHUNK,))],
        compiler_params=pltpu.CompilerParams(vmem_limit_bytes=24 * 1024 * 1024),
        cost_estimate=pl.CostEstimate(
            flops=16 * units, bytes_accessed=2 * width * units, transcendentals=0
        ),
    )(*held)
    return grad[None], b1, w2, td[None]


def solution(mesh):
    placed = (
        P(("groups", "member", "replica"), None),
        P(("groups", "member", "replica")),
        P(("groups", "member", "replica")),
        P(("groups", "member", "replica"), None),
        P(("groups", "member")),
        P(("groups", "member"), None, None),
        P(("groups", "member"), None),
        P(("groups", "member"), None),
    )
    return jax.shard_map(
        per_device,
        mesh=mesh,
        in_specs=placed,
        out_specs=(
            P(("groups", "member"), None, None),
            P(("groups", "member"), None),
            P(("groups", "member"), None),
            P(("groups", "member", "replica"), None, None),
        ),
        check_vma=False,
    )
```

```python
import functools
import math

import jax
import jax.numpy as jnp
from jax import lax
from jax.experimental import pallas as pl
from jax.experimental.pallas import tpu as pltpu
from jax.sharding import PartitionSpec as P

PEER_ROWS = 64
LANES = 128
CHUNK = 256
GROUP = 4 * PEER_ROWS

discount = 0.8


def partner(me, step, n):
    out = jnp.int32(0)
    bit = 1
    while bit < n:
        a = lax.rem(lax.div(me, jnp.int32(bit)), jnp.int32(2))
        b = lax.rem(lax.div(jnp.int32(step), jnp.int32(bit)), jnp.int32(2))
        out = out + (a + b - 2 * a * b) * bit
        bit *= 2
    return out


def kernel(
    n,
    blocks, counts, rewards, offsets, bias, head, states_hbm, w_hbm,
    grad, b1_acc, w2_acc, td,
    states, w, send, feats, aux_send, aux, err_send, err_recv,
    hid, slo, errs, acc, dpre,
    local_sem, x_send, x_recv, f_send, f_recv, a_send, a_recv, g_send, g_recv, e_send, e_recv,
):
    me = lax.axis_index("member")
    rep = lax.axis_index("replica")
    width = states_hbm.shape[2]
    hidden_units = w_hbm.shape[1]
    groups = n // 2

    load_states = pltpu.make_async_copy(states_hbm, states, local_sem.at[0])
    load_states.start()
    load_w = pltpu.make_async_copy(w_hbm, w, local_sem.at[1])
    load_w.start()

    barrier = pltpu.get_barrier_semaphore()

    def greet(step, carry):
        pl.semaphore_signal(
            barrier, inc=1, device_id={"member": partner(me, step, n)}, device_id_type=pl.DeviceIdType.MESH
        )
        return carry

    lax.fori_loop(1, n, greet, 0)
    pl.semaphore_signal(barrier, inc=1, device_id={"replica": 1 - rep}, device_id_type=pl.DeviceIdType.MESH)

    def rows_of(slot):
        return pl.ds(pl.multiple_of(slot * PEER_ROWS, PEER_ROWS), PEER_ROWS)

    def x_copy(step):
        return pltpu.make_async_remote_copy(
            src_ref=send.at[rows_of(step)], dst_ref=feats.at[rows_of(2 * step + rep)],
            send_sem=x_send.at[step], recv_sem=x_recv.at[step],
            device_id={"member": partner(me, step, n)}, device_id_type=pl.DeviceIdType.MESH,
        )

    def a_copy(step):
        return pltpu.make_async_remote_copy(
            src_ref=aux_send.at[step], dst_ref=aux.at[2 * step + rep],
            send_sem=a_send.at[step], recv_sem=a_recv.at[step],
            device_id={"member": partner(me, step, n)}, device_id_type=pl.DeviceIdType.MESH,
        )

    def f_copy(step):
        return pltpu.make_async_remote_copy(
            src_ref=feats.at[rows_of(2 * step + rep)], dst_ref=feats.at[rows_of(2 * step + rep)],
            send_sem=f_send.at[step], recv_sem=f_recv.at[step],
            device_id={"replica": 1 - rep}, device_id_type=pl.DeviceIdType.MESH,
        )

    def g_copy(step):
        return pltpu.make_async_remote_copy(
            src_ref=aux.at[2 * step + rep], dst_ref=aux.at[2 * step + rep],
            send_sem=g_send.at[step], recv_sem=g_recv.at[step],
            device_id={"replica": 1 - rep}, device_id_type=pl.DeviceIdType.MESH,
        )

    def e_copy(step, to, slot):
        return pltpu.make_async_remote_copy(
            src_ref=err_send.at[step], dst_ref=err_recv.at[slot],
            send_sem=e_send.at[step], recv_sem=e_recv.at[step],
            device_id={"member": to}, device_id_type=pl.DeviceIdType.MESH,
        )

    def picked_aux(run):
        half = lax.rem(run, jnp.int32(2))
        r = rewards[pl.ds(lax.div(run, jnp.int32(2)), 1), :]
        o = offsets[pl.ds(lax.div(run, jnp.int32(2)), 1), :].astype(jnp.float32)
        odd = jnp.full((1, LANES), half, jnp.int32) == 1
        r_other = pltpu.roll(r, PEER_ROWS, 1)
        o_other = pltpu.roll(o, PEER_ROWS, 1)
        lane = lax.broadcasted_iota(jnp.int32, (1, LANES), 1)
        row = jnp.where(
            lane < PEER_ROWS, jnp.where(odd, r_other, r), jnp.where(odd, o, o_other)
        )
        return jnp.broadcast_to(row, (8, LANES))

    def gather_aux(step, carry):
        run = blocks[0, partner(me, step, n)]
        aux_send[step] = picked_aux(run)
        return carry

    lax.fori_loop(1, n, gather_aux, 0)
    aux[rep] = picked_aux(blocks[0, me])
    load_states.wait()

    def gather(step, carry):
        run = blocks[0, partner(me, step, n)]
        send[rows_of(step), :] = states[run]
        return carry

    lax.fori_loop(1, n, gather, 0)
    feats[rows_of(rep), :] = states[blocks[0, me]]

    pl.semaphore_wait(barrier, n)

    def start_rows(i, carry):
        x_copy(i).start()
        return carry

    def aux_first(step, carry):
        a_copy(step).start()
        return carry

    lax.fori_loop(1, n, aux_first, 0)
    f_copy(0).start()
    g_copy(0).start()
    lax.fori_loop(1, n, start_rows, 0)

    b1_acc[...] = jnp.zeros_like(b1_acc)
    w2_acc[...] = jnp.zeros_like(w2_acc)
    acc[...] = jnp.zeros_like(acc)
    load_w.wait()

    def aux_forward(step, carry):
        a_copy(step).wait_recv()
        g_copy(step).start()
        return carry

    def aux_arrive(step, carry):
        g_copy(step).wait_recv()
        return carry

    lax.fori_loop(1, n, aux_forward, 0)
    lax.fori_loop(0, n, aux_arrive, 0)

    def head_group(g, slot):
        base = pl.multiple_of(g * GROUP, GROUP)
        half_group = GROUP // 2
        totals = []
        for i in range(2):
            step = 2 * g + i

            def arrive():
                x_copy(step).wait_recv()
                f_copy(step).start()

            if i == 0:
                pl.when(g > 0)(arrive)
            else:
                arrive()
            f_copy(step).wait_recv()
            here = slice(i * half_group, (i + 1) * half_group)
            x = feats[pl.ds(base + i * half_group, half_group), :]
            total = jnp.zeros((half_group, LANES), jnp.float32)
            for c in range(hidden_units // CHUNK):
                cols = slice(c * CHUNK, (c + 1) * CHUNK)
                pre = jnp.dot(x, w[:, cols], preferred_element_type=jnp.float32)
                pre = pre + bias[:, cols].astype(jnp.float32)
                hd = head[:, cols].astype(jnp.float32)
                sig = 0.5 * jnp.tanh(0.5 * pre) + 0.5
                h = pre * sig
                hid[here, cols] = h
                slo[here, cols] = (sig + h * (1.0 - sig)) * hd
                hv = h * hd
                for t in range(CHUNK // LANES):
                    total = total + hv[:, t * LANES:(t + 1) * LANES]
            totals.append(jnp.sum(total, axis=1, keepdims=True))
        value = jnp.concatenate(totals, axis=0)
        row = lax.broadcasted_iota(jnp.int32, (PEER_ROWS, LANES), 0)
        lane = lax.broadcasted_iota(jnp.int32, (PEER_ROWS, LANES), 1)
        eye = lane == row
        count = counts[0]
        e_rows = []
        for i in range(4):
            step = 2 * g + i // 2
            half = i % 2
            a = jnp.broadcast_to(aux[4 * g + i][0:1, :], (PEER_ROWS, LANES))
            v = value[i * PEER_ROWS:(i + 1) * PEER_ROWS]
            v_row = jnp.sum(jnp.where(eye, v, 0.0), axis=0, keepdims=True)
            r_col = jnp.sum(jnp.where(eye, a, 0.0), axis=1, keepdims=True)
            o_col = jnp.sum(jnp.where(lane == row + PEER_ROWS, a, 0.0), axis=1, keepdims=True)
            succ = jnp.minimum(row.astype(jnp.float32) + o_col, PEER_ROWS - 1.0)
            nxt = jnp.sum(jnp.where(lane.astype(jnp.float32) == succ, v_row, 0.0), axis=1, keepdims=True)
            factor = jnp.exp2((succ - row.astype(jnp.float32)) * math.log2(discount))
            delta = r_col + factor * nxt - v
            q = (half * n + partner(me, step, n)) * PEER_ROWS + row
            err = jnp.where(q < count, delta, 0.0)
            errs[i * PEER_ROWS:(i + 1) * PEER_ROWS, :] = err
            e_rows.append(jnp.sum(jnp.where(eye, err, 0.0), axis=0, keepdims=True))
        mine = jnp.full((8, LANES), rep, jnp.int32) == 0
        for i in range(2):
            err_send[2 * g + i] = jnp.where(mine, e_rows[2 * i], e_rows[2 * i + 1])
        for i in range(2):
            step = 2 * g + i

            def start_err():
                e_copy(step, partner(me, step, n), me).start()

            if i == 0:
                pl.when(g > 0)(start_err)
            else:
                start_err()
        for t in range(hidden_units // LANES):
            cols = slice(t * LANES, (t + 1) * LANES)
            neg = -errs[...]
            dp = neg * slo[:, cols]
            dpre[slot * GROUP:(slot + 1) * GROUP, cols] = dp.astype(jnp.bfloat16)
            b1_acc[:, cols] += jnp.sum(dp.reshape(GROUP // 8, 8, LANES), axis=0)
            gw = neg * hid[:, cols]
            w2_acc[:, cols] += jnp.sum(gw.reshape(GROUP // 8, 8, LANES), axis=0)

    def grad_chunk(g, k, rows):
        base = pl.multiple_of(g * GROUP, GROUP)
        cols = pl.ds(pl.multiple_of(k * CHUNK, CHUNK), CHUNK)
        return lax.dot_general(
            feats[pl.ds(base, rows), cols], dpre[:rows, :],
            (((0,), (0,)), ((), ())), preferred_element_type=jnp.float32,
        )

    def out_rows(k):
        return pl.ds(pl.multiple_of(k * CHUNK, CHUNK), CHUNK)

    def middle(g, carry):
        head_group(g, 0)

        def add(k, c):
            acc[out_rows(k), :] += grad_chunk(g, k, GROUP)
            return c

        lax.fori_loop(0, width // CHUNK, add, 0)
        return carry

    lax.fori_loop(0, groups - 2, middle, 0)
    before = jnp.int32(groups - 2)
    head_group(before, 0)
    head_group(jnp.int32(groups - 1), 1)

    def finish(k, c):
        grad[out_rows(k), :] = (acc[out_rows(k), :] + grad_chunk(before, k, 2 * GROUP)).astype(jnp.bfloat16)
        return c

    lax.fori_loop(0, width // CHUNK, finish, 0)

    def drain(step, carry):
        x_copy(step).wait_send()
        a_copy(step).wait_send()
        e_copy(step, partner(me, step, n), me).wait()
        return carry

    lax.fori_loop(1, n, drain, 0)

    def drain_forward(step, carry):
        f_copy(step).wait_send()
        g_copy(step).wait_send()
        return carry

    lax.fori_loop(0, n, drain_forward, 0)
    err_recv[me] = err_send[0]
    for m in range(n):
        td[m:m + 1, :] = err_recv[m][0:1, :PEER_ROWS]


def final_kernel(grad, b1_acc, w2_acc, td_in, grad_hbm, grad_b1, grad_w2, td, out_sem):
    steps = grad.shape[0] // CHUNK

    def out_copy(k):
        rows = slice(k * CHUNK, (k + 1) * CHUNK)
        return pltpu.make_async_copy(grad.at[rows], grad_hbm.at[rows], out_sem.at[k])

    for k in range(steps):
        out_copy(k).start()
    grad_b1[...] = jnp.sum(b1_acc[...], axis=0, keepdims=True)
    grad_w2[...] = jnp.sum(w2_acc[...], axis=0, keepdims=True)
    td[...] = td_in[...]
    for k in range(steps):
        out_copy(k).wait()


def per_device(states, rewards, offsets, blocks, counts, w_first, b_first, w_value):
    n = lax.axis_size("member")
    rows, width = states.shape
    units = w_first.shape[2]
    runs = rows // PEER_ROWS
    vmem = pl.BlockSpec(memory_space=pltpu.VMEM)
    smem = pl.BlockSpec(memory_space=pltpu.SMEM)
    hbm = pl.BlockSpec(memory_space=pltpu.HBM)
    f32, bf16 = jnp.float32, jnp.bfloat16
    dma = pltpu.SemaphoreType.DMA
    limit = 60 * 2**20
    held = pl.pallas_call(
        functools.partial(kernel, n),
        out_shape=(
            pltpu.VMEM((width, units), bf16),
            pltpu.VMEM((8, units), f32),
            pltpu.VMEM((8, units), f32),
            pltpu.VMEM((n, PEER_ROWS), f32),
        ),
        in_specs=[smem, smem, vmem, vmem, vmem, vmem, hbm, hbm],
        out_specs=(vmem,) * 4,
        scratch_shapes=[
            pltpu.VMEM((runs, PEER_ROWS, width), bf16),
            pltpu.VMEM((width, units), bf16),
            pltpu.VMEM((n * PEER_ROWS, width), bf16),
            pltpu.VMEM((2 * n * PEER_ROWS, width), bf16),
            pltpu.VMEM((n, 8, LANES), f32),
            pltpu.VMEM((2 * n, 8, LANES), f32),
            pltpu.VMEM((n, 8, LANES), f32),
            pltpu.VMEM((n, 8, LANES), f32),
            pltpu.VMEM((GROUP, units), f32),
            pltpu.VMEM((GROUP, units), f32),
            pltpu.VMEM((GROUP, LANES), f32),
            pltpu.VMEM((width, units), f32),
            pltpu.VMEM((2 * GROUP, units), bf16),
            dma((2,)),
            dma((n,)), dma((n,)), dma((n,)), dma((n,)), dma((n,)), dma((n,)),
            dma((n,)), dma((n,)), dma((n,)), dma((n,)),
        ],
        compiler_params=pltpu.CompilerParams(
            collective_id=0, has_side_effects=True, vmem_limit_bytes=limit,
        ),
        cost_estimate=pl.CostEstimate(
            flops=8 * n * PEER_ROWS * width * units,
            bytes_accessed=2 * (rows * width + 2 * width * units),
            transcendentals=2 * n * PEER_ROWS * units,
        ),
    )(
        blocks, counts, rewards.reshape(-1, LANES), offsets.reshape(-1, LANES),
        b_first, w_value, states.reshape(runs, PEER_ROWS, width), w_first[0],
    )
    grad, b1, w2, td = pl.pallas_call(
        final_kernel,
        out_shape=(
            jax.ShapeDtypeStruct((width, units), bf16),
            jax.ShapeDtypeStruct((1, units), f32),
            jax.ShapeDtypeStruct((1, units), f32),
            jax.ShapeDtypeStruct((n, PEER_ROWS), f32),
        ),
        in_specs=[vmem] * 4,
        out_specs=(hbm, vmem, vmem, vmem),
        scratch_shapes=[dma((width // CHUNK,))],
        compiler_params=pltpu.CompilerParams(vmem_limit_bytes=24 * 1024 * 1024),
        cost_estimate=pl.CostEstimate(
            flops=16 * units, bytes_accessed=2 * width * units, transcendentals=0
        ),
    )(*held)
    return grad[None], b1, w2, td[None]


def solution(mesh):
    placed = (
        P(("groups", "member", "replica"), None),
        P(("groups", "member", "replica")),
        P(("groups", "member", "replica")),
        P(("groups", "member", "replica"), None),
        P(("groups", "member")),
        P(("groups", "member"), None, None),
        P(("groups", "member"), None),
        P(("groups", "member"), None),
    )
    return jax.shard_map(
        per_device,
        mesh=mesh,
        in_specs=placed,
        out_specs=(
            P(("groups", "member"), None, None),
            P(("groups", "member"), None),
            P(("groups", "member"), None),
            P(("groups", "member", "replica"), None, None),
        ),
        check_vma=False,
    )
```
